1024 devices in a mesh: dp: 4 (over x), pipe: 8 (over y, core), ctx: 32 (over z).
Axes of the slice: x: 4, y: 4, z: 32, core: 2. Of those that a mesh axis runs over, the one named last changes fastest.
Arguments:
- activations: bfloat16 [4, 8, 3, 32, 262144], P('dp', 'pipe', None, None, 'ctx'), may hold values from -16 to 16
- cotangents: bfloat16 [4, 8, 32, 262144], P('dp', 'pipe', None, 'ctx'), may hold values from -3 to 3
- norm_gains: float32 [8, 2, 32, 64], P('pipe', None, 'ctx'), may hold values from 0.6 to 6.6
- key_blocks: int32 [8, 32, 32, 2], P('pipe', 'ctx'), may hold values from 0 to 32, as said below
Outputs:
- attended: bfloat16 [4, 8, 32, 262144], P('dp', 'pipe', None, 'ctx')
- gain_grads: float32 [8, 2, 32, 64], P('pipe', None, 'ctx')
The draws below stay inside these ranges and needn't reach their ends.
Inputs may be any that keep to these rules, and one draw needn't show every extreme that they name: `key_blocks`: each row lists distinct key blocks and always its own block first; unused slots hold 32 and stand after the used ones; rows hold different numbers of blocks.
All inputs are finite; a program needn't handle non-finite values.
Results may differ from the reference program's by a relative error of at most 0.0035.
The reference program's roundings to bfloat16 on the way (of `arrived`, `returned` and `grad_scores`) count: a program that leaves them out, or rounds other values in their place, can miss the bound.
Values may be sent and summed in bfloat16 or wider, within the bound.
A program may use at most 32 MiB of HBM per device.

```python
import math
import jax
import jax.numpy as jnp
from jax import lax

HEADS = 32
HEAD_DIM = 64
BLOCK = 128
SEQ = 4096
BLOCKS = 32
SLOTS = 2
N_DP = 4
N_PIPE = 8


def draw_activations(key, part):
    base_key = jax.random.fold_in(key, 3)
    noise_key, row_key, col_key = jax.random.split(base_key, 3)
    full_shape = (N_DP, N_PIPE, 3, HEADS, SEQ, HEAD_DIM)
    base = jnp.clip(jax.random.normal(noise_key, full_shape, jnp.float32), -3.0, 3.0)
    row_scale = jnp.exp(jax.random.uniform(row_key, full_shape[:5] + (1,), jnp.float32, math.log(0.5), math.log(2.0)))
    col_scale = jnp.exp(jax.random.uniform(col_key, (1, 1, 3, HEADS, 1, HEAD_DIM), jnp.float32, math.log(0.5), math.log(2.0)))
    values = base * row_scale * col_scale
    return values.reshape(N_DP, N_PIPE, 3, HEADS, SEQ * HEAD_DIM).astype(jnp.bfloat16)


def draw_norm_gains(key, part):
    base_key = jax.random.fold_in(key, 5)
    first_key = jax.random.fold_in(base_key, 0)
    return jnp.exp(jax.random.uniform(first_key, (N_PIPE, 2, HEADS, HEAD_DIM), jnp.float32, math.log(0.6), math.log(2.2)))


def draw_key_blocks(key, part):
    base_key = jax.random.fold_in(key, 11)
    total_rows = N_PIPE * HEADS * BLOCKS
    row_keys = jax.random.split(base_key, total_rows)
    row_pos = jnp.arange(total_rows, dtype=jnp.int32) % BLOCKS

    def one_row(row_key, position):
        kind_key, other_key = jax.random.split(row_key)
        kind = jax.random.randint(kind_key, (), 0, 4, dtype=jnp.int32)
        kind = jnp.where(position == BLOCKS // 2, 1 + kind % 3, kind)
        kind = jnp.where(position == BLOCKS - 1, 0, kind)
        other = jax.random.randint(other_key, (), 0, BLOCKS - 1, dtype=jnp.int32)
        other = other + (other >= position).astype(jnp.int32)
        has_earlier = position > 0
        extra = jnp.where((kind == 1) & has_earlier, position - 1, jnp.where((kind == 2) & has_earlier, 0, other))
        extra = jnp.where(kind == 0, BLOCKS, extra)
        return jnp.stack([position, extra]).astype(jnp.int32)
    table = jax.vmap(one_row)(row_keys, row_pos)
    return table.reshape(N_PIPE, HEADS, BLOCKS, SLOTS)


def block_scale(key, dims, pieces, low, largest):
    def one(dim, blocks):
        draws = jax.random.uniform(jax.random.fold_in(jax.random.fold_in(key, 6), dim), (blocks,), jnp.float32, low / len(pieces), largest / len(pieces))
        return jnp.repeat(jnp.exp(draws), dims[dim] // blocks).reshape((-1,) + (1,) * (len(dims) - dim - 1))

    level = one(*pieces[0])
    for cut in pieces[1:]:
        level = level * one(*cut)
    return level


def centred(key, shape, scale, limit, shards=(), kind=jnp.bfloat16):
    values = jax.random.normal(key, shape, jnp.float32) * scale
    if len(shards) > 0:
        values = block_scale(key, shape, shards, -0.22, 0.18) * values
    return jnp.clip(values, min=-limit, max=limit).astype(kind)


def setup_inputs(seed: int = 0) -> dict:
    splits = jax.random.split(jax.random.key(seed), 5)
    activations = draw_activations(jax.random.fold_in(splits[4], 71), 0)
    cotangents = centred(splits[1], (N_DP, N_PIPE, HEADS, SEQ * HEAD_DIM), 0.5, 3.0, ((0, 4), (1, 8), (3, 32)))
    norm_gains = draw_norm_gains(jax.random.fold_in(splits[4], 71), 0)
    key_blocks = draw_key_blocks(jax.random.fold_in(splits[4], 71), 0)
    return {"activations": activations, "cotangents": cotangents, "norm_gains": norm_gains, "key_blocks": key_blocks}


EPS = 1e-06

def rounded(array):
    return lax.optimization_barrier(array.astype(jnp.bfloat16)).astype(jnp.float32)

def normalize(raw_vals, gain_row):
    vals_f = raw_vals.astype(jnp.float32)
    unit_rows = vals_f * lax.rsqrt(lax.optimization_barrier(jnp.mean(vals_f * vals_f, axis=-1, keepdims=True)) + EPS)
    return (unit_rows, rounded(unit_rows * gain_row))

def head_pass(query_raw, key_raw, value_raw, cotangent, gain_query, gain_key, block_list):
    score_scale = HEAD_DIM ** (-0.5)
    q_unit, q_normed = normalize(query_raw, gain_query)
    k_unit, k_normed = normalize(key_raw, gain_key)
    live_slots = block_list < BLOCKS
    safe_idx = jnp.where(live_slots, block_list, 0).astype(jnp.int32)

    def tiles(field):
        blocked = field.reshape(BLOCKS, BLOCK, HEAD_DIM)
        return blocked[safe_idx].reshape(BLOCKS, SLOTS * BLOCK, HEAD_DIM)
    k_tiles = tiles(k_normed)
    v_tiles = tiles(value_raw.astype(jnp.float32))
    unit_tiles = tiles(k_unit)
    q_blocks = q_normed.reshape(BLOCKS, BLOCK, HEAD_DIM)
    scores = jnp.einsum('nqd,nkd->nqk', q_blocks, k_tiles) * score_scale
    key_mask = jnp.repeat(live_slots, BLOCK, axis=1)[:, None, :]
    scores = jnp.where(key_mask, scores, -jnp.inf)
    row_max = lax.optimization_barrier(jnp.max(scores, axis=-1, keepdims=True))
    exp_rows = jnp.exp(scores - row_max)
    prob_rows = exp_rows / lax.optimization_barrier(jnp.sum(exp_rows, axis=-1, keepdims=True))
    attended_f32 = jnp.einsum('nqk,nkd->nqd', rounded(prob_rows), v_tiles)
    attended = attended_f32.astype(jnp.bfloat16)
    grad_blocks = cotangent.astype(jnp.float32).reshape(BLOCKS, BLOCK, HEAD_DIM)
    grad_probs = jnp.einsum('nqd,nkd->nqk', grad_blocks, v_tiles)
    row_dot = lax.optimization_barrier(jnp.sum(grad_blocks * attended_f32, axis=-1, keepdims=True))
    grad_scores = rounded(prob_rows * (grad_probs - row_dot) * score_scale)
    grad_query = jnp.einsum('nqk,nkd->nqd', grad_scores, k_tiles)
    grad_key = jnp.einsum('nqk,nqd->nkd', grad_scores, q_blocks)
    query_gain = lax.optimization_barrier(jnp.sum(grad_query * q_unit.reshape(BLOCKS, BLOCK, HEAD_DIM), axis=(0, 1)))
    key_gain = lax.optimization_barrier(jnp.sum(grad_key * unit_tiles, axis=(0, 1)))
    return (attended.reshape(SEQ * HEAD_DIM), jnp.stack([query_gain, key_gain]))

def reference(activations, cotangents, norm_gains, key_blocks):

    def one_section(flat_idx):
        replica = flat_idx // N_PIPE
        section_idx = flat_idx % N_PIPE
        source = (section_idx + N_PIPE - 1) % N_PIPE
        following = (section_idx + 1) % N_PIPE
        arrived = activations[replica, source]
        returned = cotangents[replica, following]
        gain_pair = norm_gains[section_idx]
        block_table = key_blocks[section_idx]

        def one_head(head_idx):
            fields = arrived[:, head_idx].reshape(3, SEQ, HEAD_DIM)
            return head_pass(fields[0], fields[1], fields[2], returned[head_idx].reshape(SEQ, HEAD_DIM), gain_pair[0, head_idx], gain_pair[1, head_idx], block_table[head_idx])
        outputs, gain_terms = lax.map(one_head, jnp.arange(HEADS, dtype=jnp.int32))
        return (outputs, jnp.transpose(gain_terms, (1, 0, 2)))
    outputs, gain_terms = lax.map(one_section, jnp.arange(N_DP * N_PIPE, dtype=jnp.int32))
    attended = outputs.reshape(N_DP, N_PIPE, HEADS, SEQ * HEAD_DIM)
    gain_grads = lax.optimization_barrier(jnp.sum(gain_terms.reshape(N_DP, N_PIPE, 2, HEADS, HEAD_DIM), axis=0))
    return (attended, gain_grads)
```

```python
import jax
import jax.numpy as jnp
from jax import lax
from jax.experimental import pallas as pl
from jax.experimental.pallas import tpu as pltpu
from jax.sharding import PartitionSpec as P

HEADS = 32
DIM = 64
BLOCKS = 32
ROWS = 64
EPS = 1e-06
F32 = jnp.float32
BF16 = jnp.bfloat16


def from_behind(value, axis, steps):
    count = lax.axis_size(axis)
    pairs = [(source, (source + steps) % count) for source in range(count)]
    return lax.ppermute(value, axis, pairs)


def dims_by_tokens(pairs):
    turned = pairs.astype(F32).T
    return jnp.concatenate([turned[:DIM], turned[DIM:]], axis=1)


def rows_of_pairs(turned):
    return jnp.concatenate([turned[:, :DIM], turned[:, DIM:]], axis=0).T


def contract(left, right, left_dim, right_dim):
    return lax.dot_general(
        left, right, (((left_dim,), (right_dim,)), ((), ())), preferred_element_type=F32
    )


def unit(vals):
    return vals * lax.rsqrt(jnp.mean(vals * vals, axis=0, keepdims=True) + EPS)


def one_head(query, key, value, grad, other_key, other_value, gain_row, live_row):
    scale = DIM ** (-0.5)
    gains = jnp.broadcast_to(gain_row, (2 * DIM, 2 * DIM)).T
    query_gain, key_gain = gains[:DIM], gains[DIM:]
    q_unit = unit(dims_by_tokens(query))
    k_unit = unit(dims_by_tokens(key))
    o_unit = unit(dims_by_tokens(other_key))
    q_normed = (q_unit * query_gain).astype(BF16)
    k_normed = jnp.concatenate([k_unit * key_gain, o_unit * key_gain], axis=1).astype(BF16)
    values = jnp.concatenate(
        [dims_by_tokens(value), dims_by_tokens(other_value)], axis=1
    ).astype(BF16)
    grad_f = dims_by_tokens(grad)
    scores = contract(k_normed, q_normed, 0, 0) * scale
    own_scores = scores[:128]
    other_scores = jnp.where(live_row > 0.5, scores[128:], -jnp.inf)
    row_max = jnp.maximum(
        jnp.max(own_scores, axis=0, keepdims=True), jnp.max(other_scores, axis=0, keepdims=True)
    )
    exp_own = jnp.exp(own_scores - row_max)
    exp_other = jnp.exp(other_scores - row_max)
    row_sum = jnp.sum(exp_own, axis=0, keepdims=True) + jnp.sum(exp_other, axis=0, keepdims=True)
    probs = jnp.concatenate([exp_own, exp_other], axis=0) / row_sum
    attended = contract(values, probs.astype(BF16), 1, 0)
    grad_probs = contract(values, grad_f.astype(BF16), 0, 0)
    row_dot = jnp.sum(grad_f * attended, axis=0, keepdims=True)
    grad_scores = (probs * (grad_probs - row_dot) * scale).astype(BF16)
    grad_query = contract(k_normed, grad_scores, 1, 0)
    grad_key = contract(q_normed, grad_scores, 1, 1)
    query_col = jnp.sum(grad_query * q_unit, axis=1, keepdims=True)
    key_col = jnp.sum(
        grad_key[:, :128] * k_unit + grad_key[:, 128:] * o_unit, axis=1, keepdims=True
    )
    return rows_of_pairs(attended).astype(BF16), jnp.concatenate([query_col, key_col], axis=0)


def attention_kernel(qkv_ref, grad_ref, other_ref, gain_ref, live_ref, out_ref, gain_out_ref):
    lane = lax.broadcasted_iota(jnp.int32, (2 * DIM, 128), 1)

    def step(head, totals):
        out, col = one_head(
            qkv_ref[0, head],
            qkv_ref[1, head],
            qkv_ref[2, head],
            grad_ref[head],
            other_ref[head, 0],
            other_ref[head, 1],
            gain_ref[head],
            live_ref[head],
        )
        out_ref[head] = out
        return jnp.where(lane == head, col, totals)

    totals = lax.fori_loop(0, HEADS, step, jnp.zeros((2 * DIM, 128), F32))
    gain_out_ref[...] = totals.T[:HEADS]


def attention(qkv, grads, others, gains, live):
    return pl.pallas_call(
        attention_kernel,
        out_shape=(
            jax.ShapeDtypeStruct((HEADS, ROWS, 128), BF16),
            jax.ShapeDtypeStruct((HEADS, 128), F32),
        ),
        in_specs=[pl.BlockSpec(memory_space=pltpu.VMEM)] * 5,
        out_specs=(pl.BlockSpec(memory_space=pltpu.VMEM),) * 2,
        compiler_params=pltpu.CompilerParams(vmem_limit_bytes=24 * 2**20),
    )(qkv, grads, others, gains, live)


def local(activations, cotangents, norm_gains, key_blocks):
    qkv = from_behind(activations[0, 0].reshape(3, HEADS, ROWS, 128), "pipe", 1)
    grads = from_behind(cotangents[0, 0].reshape(HEADS, ROWS, 128), "pipe", -1)
    table = key_blocks[0, 0]
    gain_rows = lax.all_gather(norm_gains[0].reshape(1, 1, 128), "ctx", axis=0, tiled=True)
    lists = lax.all_gather(table[None, :, 1], "ctx", axis=0, tiled=True)
    live = (lists[:, lax.axis_index("ctx")] < BLOCKS).astype(F32)
    live_rows = jnp.broadcast_to(live[:, None, None], (HEADS, 1, 128))
    keys_values = jnp.swapaxes(qkv[1:], 0, 1)
    held = lax.all_to_all(keys_values, "ctx", split_axis=0, concat_axis=0, tiled=True)
    listed = jnp.where(table[:, 1] < BLOCKS, table[:, 1], 0)
    picked = jnp.take(held, listed, axis=0)
    others = lax.all_to_all(picked, "ctx", split_axis=0, concat_axis=0, tiled=True)
    out, terms = attention(qkv, grads, others, gain_rows, live_rows)
    summed = lax.psum(lax.psum_scatter(terms, "ctx", scatter_dimension=0, tiled=True), "dp")
    return out.reshape(1, 1, HEADS, ROWS * 128), summed.reshape(1, 2, 1, DIM)


def solution(mesh):
    return jax.shard_map(
        local,
        mesh=mesh,
        in_specs=(
            P("dp", "pipe", None, None, "ctx"),
            P("dp", "pipe", None, "ctx"),
            P("pipe", None, "ctx", None),
            P("pipe", "ctx", None, None),
        ),
        out_specs=(P("dp", "pipe", None, "ctx"), P("pipe", None, "ctx", None)),
        check_vma=False,
    )
```

```python
import jax
import jax.numpy as jnp
from jax import lax
from jax.experimental import pallas as pl
from jax.experimental.pallas import tpu as pltpu
from jax.sharding import PartitionSpec as P

DIM = 64
ROWS = 64
EPS = 1e-06
F32 = jnp.float32
BF16 = jnp.bfloat16
MESH = pl.DeviceIdType.MESH


def dims_by_tokens(pairs):
    turned = pairs.astype(F32).T
    return jnp.concatenate([turned[:DIM], turned[DIM:]], axis=1)


def rows_of_pairs(turned):
    return jnp.concatenate([turned[:, :DIM], turned[:, DIM:]], axis=0).T


def contract(left, right, left_dim, right_dim):
    return lax.dot_general(
        left, right, (((left_dim,), (right_dim,)), ((), ())), preferred_element_type=F32
    )


def unit(vals):
    return vals * lax.rsqrt(jnp.mean(vals * vals, axis=0, keepdims=True) + EPS)


def one_head(query, key, value, grad, other_key, other_value, gain_row, live_row):
    scale = DIM ** (-0.5)
    gains = jnp.broadcast_to(gain_row, (2 * DIM, 2 * DIM)).T
    query_gain, key_gain = gains[:DIM], gains[DIM:]
    q_unit = unit(dims_by_tokens(query))
    k_unit = unit(dims_by_tokens(key))
    o_unit = unit(dims_by_tokens(other_key))
    q_normed = (q_unit * query_gain).astype(BF16)
    k_normed = jnp.concatenate([k_unit * key_gain, o_unit * key_gain], axis=1).astype(BF16)
    values = jnp.concatenate(
        [dims_by_tokens(value), dims_by_tokens(other_value)], axis=1
    ).astype(BF16)
    grad_f = dims_by_tokens(grad)
    scores = contract(k_normed, q_normed, 0, 0) * scale
    own_scores = scores[:128]
    other_scores = jnp.where(live_row > 0.5, scores[128:], -jnp.inf)
    row_max = jnp.maximum(
        jnp.max(own_scores, axis=0, keepdims=True), jnp.max(other_scores, axis=0, keepdims=True)
    )
    exp_own = jnp.exp(own_scores - row_max)
    exp_other = jnp.exp(other_scores - row_max)
    row_sum = jnp.sum(exp_own, axis=0, keepdims=True) + jnp.sum(exp_other, axis=0, keepdims=True)
    probs = jnp.concatenate([exp_own, exp_other], axis=0) / row_sum
    attended = contract(values, probs.astype(BF16), 1, 0)
    grad_probs = contract(values, grad_f.astype(BF16), 0, 0)
    row_dot = jnp.sum(grad_f * attended, axis=0, keepdims=True)
    grad_scores = (probs * (grad_probs - row_dot) * scale).astype(BF16)
    grad_query = contract(k_normed, grad_scores, 1, 0)
    grad_key = contract(q_normed, grad_scores, 1, 1)
    query_col = jnp.sum(grad_query * q_unit, axis=1, keepdims=True)
    key_col = jnp.sum(
        grad_key[:, :128] * k_unit + grad_key[:, 128:] * o_unit, axis=1, keepdims=True
    )
    return rows_of_pairs(attended).astype(BF16), jnp.concatenate([query_col, key_col], axis=0)


def step_offset(step):
    return ((step + 1) // 2) * (2 * (step % 2) - 1)


def relay_kernel(
    table_ref, gain_ref, qkv_ref, grad_ref, out_ref, sums_ref,
    own_qkv, own_grad, held, picked, others, notes_out, notes,
    terms_out, terms, totals_out, totals,
    own_send, own_recv, grad_send, grad_recv, held_send, held_recv,
    other_send, other_recv, note_send, note_recv,
    term_send, term_recv, total_send, total_recv,
):
    n = held.shape[0]
    replicas = totals.shape[0]
    stages = lax.axis_size("pipe")
    d, p, z = lax.axis_index("dp"), lax.axis_index("pipe"), lax.axis_index("ctx")
    ahead = lax.rem(p + 1, stages)
    behind = lax.rem(p + stages - 1, stages)

    def partner(step):
        return lax.rem(z + step_offset(step) + n, n)

    def remote(src, dst, send, recv, target):
        return pltpu.make_async_remote_copy(
            src_ref=src, dst_ref=dst, send_sem=send, recv_sem=recv,
            device_id=target, device_id_type=MESH,
        )

    barrier = pltpu.get_barrier_semaphore()

    def greet(step, carry):
        other = partner(step)
        pl.semaphore_signal(barrier, inc=1, device_id=(d, ahead, other), device_id_type=MESH)
        pl.semaphore_signal(barrier, inc=1, device_id=(d, behind, other), device_id_type=MESH)

        @pl.when(step > 0)
        def _():
            pl.semaphore_signal(barrier, inc=1, device_id=(d, p, other), device_id_type=MESH)

        return carry

    lax.fori_loop(0, n, greet, 0)
    for hop in range(1, replicas):
        pl.semaphore_signal(
            barrier, inc=1, device_id=(lax.rem(d + hop, replicas), p, z), device_id_type=MESH
        )

    def write_note(block, carry):
        live = jnp.where(table_ref[2 * block + 1] < n, 1.0, 0.0).astype(F32)
        notes_out[block, 0:1, :] = gain_ref[...]
        notes_out[block, 1:2, :] = jnp.full((1, 128), live, F32)
        return carry

    lax.fori_loop(0, n, write_note, 0)
    notes[z] = notes_out[z]
    pl.semaphore_wait(barrier, 3 * n - 1 + replicas - 1)

    def send_note(step, carry):
        other = partner(step)
        remote(notes_out.at[other], notes.at[z], note_send, note_recv, (d, p, other)).start()
        return carry

    def send_to_owner(step, carry):
        other = partner(step)
        remote(
            qkv_ref.at[pl.ds(1, 2), other], held.at[z], held_send, held_recv, (d, ahead, other)
        ).start()
        return carry

    lax.fori_loop(1, n, send_note, 0)
    lax.fori_loop(0, n, send_to_owner, 0)
    own_copy = remote(qkv_ref, own_qkv, own_send, own_recv, (d, ahead, z))
    own_copy.start()
    grad_copy = remote(grad_ref, own_grad, grad_send, grad_recv, (d, behind, z))
    grad_copy.start()

    all_held = remote(held, held, held_send, held_recv, (d, ahead, z))
    all_held.wait_recv()

    def pick(block):
        listed = table_ref[2 * block + 1]
        return held[jnp.where(listed < n, listed, 0)]

    others[z] = pick(z)

    def send_picked(step, carry):
        other = partner(step)
        picked[other] = pick(other)
        remote(
            picked.at[other], others.at[z], other_send, other_recv.at[z], (d, p, other)
        ).start()
        return carry

    lax.fori_loop(1, n, send_picked, 0)
    own_copy.wait_recv()
    grad_copy.wait_recv()
    rest = pl.ds(0, n - 1)
    all_notes = remote(notes_out.at[rest], notes.at[rest], note_send, note_recv, (d, p, z))
    all_notes.wait_recv()
    lane = lax.broadcasted_iota(jnp.int32, (2 * DIM, 128), 1)

    def attend(step, sums):
        head = partner(step)

        @pl.when(step > 0)
        def _():
            remote(
                picked.at[head], others.at[head], other_send, other_recv.at[head], (d, p, head)
            ).wait_recv()

        out, col = one_head(
            own_qkv[0, head], own_qkv[1, head], own_qkv[2, head], own_grad[head],
            others[head, 0], others[head, 1], notes[head, 0:1, :], notes[head, 1:2, :],
        )
        out_ref[head] = out
        return jnp.where(lane == head, col, sums)

    sums = lax.fori_loop(0, n, attend, jnp.zeros((2 * DIM, 128), F32)).T
    for head in range(n):
        terms_out[head] = sums[head : head + 1]
    terms[z] = terms_out[z]

    def send_terms(step, carry):
        other = partner(step)
        remote(terms_out.at[other], terms.at[z], term_send, term_recv, (d, p, other)).start()
        return carry

    lax.fori_loop(1, n, send_terms, 0)
    all_terms = remote(terms_out.at[rest], terms.at[rest], term_send, term_recv, (d, p, z))
    all_terms.wait_recv()
    total = jnp.sum(terms[...], axis=0)
    totals[d] = total
    totals_out[...] = total
    for hop in range(1, replicas):
        remote(
            totals_out, totals.at[d], total_send, total_recv,
            (lax.rem(d + hop, replicas), p, z),
        ).start()
    rows = pl.ds(0, replicas - 1)
    all_totals = remote(totals.at[rows], totals.at[rows], total_send, total_recv, (d, p, z))
    all_totals.wait_recv()
    sums_ref[...] = jnp.sum(totals[...], axis=0)
    own_copy.wait_send()
    grad_copy.wait_send()
    all_held.wait_send()
    all_notes.wait_send()
    remote(picked.at[rest], picked.at[rest], other_send, other_recv.at[z], (d, p, z)).wait_send()
    all_terms.wait_send()
    all_totals.wait_send()


def relay(table, gains, qkv, grads):
    n = grads.shape[0]
    replicas = lax.axis_size("dp")
    dma = pltpu.SemaphoreType.DMA
    block = (ROWS, 128)
    vmem = pl.BlockSpec(memory_space=pltpu.VMEM)
    return pl.pallas_call(
        relay_kernel,
        out_shape=(
            jax.ShapeDtypeStruct((n,) + block, BF16),
            jax.ShapeDtypeStruct((1, 128), F32),
        ),
        in_specs=[pl.BlockSpec(memory_space=pltpu.SMEM), vmem, vmem, vmem],
        out_specs=(vmem, vmem),
        scratch_shapes=[
            pltpu.VMEM((3, n) + block, BF16),
            pltpu.VMEM((n,) + block, BF16),
            pltpu.VMEM((n, 2) + block, BF16),
            pltpu.VMEM((n, 2) + block, BF16),
            pltpu.VMEM((n, 2) + block, BF16),
            pltpu.VMEM((n, 2, 128), F32),
            pltpu.VMEM((n, 2, 128), F32),
            pltpu.VMEM((n, 1, 128), F32),
            pltpu.VMEM((n, 1, 128), F32),
            pltpu.VMEM((1, 128), F32),
            pltpu.VMEM((replicas, 1, 128), F32),
            dma, dma, dma, dma, dma, dma,
            dma, dma((n,)), dma, dma,
            dma, dma, dma, dma,
        ],
        compiler_params=pltpu.CompilerParams(
            collective_id=0, has_side_effects=True, vmem_limit_bytes=32 * 2**20
        ),
        cost_estimate=pl.CostEstimate(
            flops=n * 10 * 128 * 256 * DIM, bytes_accessed=n * 10 * 2**14,
            transcendentals=n * 256 * 128,
        ),
    )(table, gains, qkv, grads)


def local(activations, cotangents, norm_gains, key_blocks):
    heads = activations.shape[3]
    qkv = activations.reshape(3, heads, ROWS, 128)
    grads = cotangents.reshape(heads, ROWS, 128)
    out, sums = relay(key_blocks.reshape(-1), norm_gains.reshape(1, 128), qkv, grads)
    return out.reshape(1, 1, heads, ROWS * 128), sums.reshape(1, 2, 1, DIM)


def solution(mesh):
    return jax.shard_map(
        local,
        mesh=mesh,
        in_specs=(
            P("dp", "pipe", None, None, "ctx"),
            P("dp", "pipe", None, "ctx"),
            P("pipe", None, "ctx", None),
            P("pipe", "ctx", None, None),
        ),
        out_specs=(P("dp", "pipe", None, "ctx"), P("pipe", None, "ctx", None)),
        check_vma=False,
    )
```

```python
import jax
import jax.numpy as jnp
from jax import lax
from jax.experimental import pallas as pl
from jax.experimental.pallas import tpu as pltpu
from jax.sharding import PartitionSpec as P

DIM = 64
SCALE = DIM ** (-0.5)
ROWS = 64
EPS = 1e-06
F32 = jnp.float32
BF16 = jnp.bfloat16
MESH = pl.DeviceIdType.MESH


def dims_by_tokens(pairs):
    turned = pairs.astype(F32).T
    return jnp.concatenate([turned[:DIM], turned[DIM:]], axis=1)


def rows_of_pairs(turned):
    return jnp.concatenate([turned[:, :DIM], turned[:, DIM:]], axis=0).T


def contract(left, right, left_dim, right_dim):
    return lax.dot_general(
        left, right, (((left_dim,), (right_dim,)), ((), ())), preferred_element_type=F32
    )


def unit(vals):
    return vals * lax.rsqrt(jnp.mean(vals * vals, axis=0, keepdims=True) + EPS)


def prepare_head(query, key, value, grad, gain_row):
    gains = jnp.broadcast_to(gain_row, (2 * DIM, 2 * DIM)).T
    q_unit = unit(dims_by_tokens(query))
    k_unit = unit(dims_by_tokens(key))
    q_normed = (q_unit * gains[:DIM]).astype(BF16)
    k_normed = (k_unit * gains[DIM:]).astype(BF16)
    values = dims_by_tokens(value).astype(BF16)
    grad_t = dims_by_tokens(grad).astype(BF16)
    scores = contract(k_normed, q_normed, 0, 0) * SCALE
    grad_probs = contract(values, grad_t, 0, 0)
    return q_unit, k_unit, gains[DIM:], q_normed, k_normed, values, grad_t, scores, grad_probs


def weigh_head(other_key, key_gain, q_normed, own_scores, own_values, live_row):
    o_unit = unit(dims_by_tokens(other_key))
    o_normed = (o_unit * key_gain).astype(BF16)
    other_scores = contract(o_normed, q_normed, 0, 0) * SCALE
    other_scores = jnp.where(live_row > 0.5, other_scores, -jnp.inf)
    row_max = jnp.maximum(
        jnp.max(own_scores, axis=0, keepdims=True), jnp.max(other_scores, axis=0, keepdims=True)
    )
    exp_own = jnp.exp(own_scores - row_max)
    exp_other = jnp.exp(other_scores - row_max)
    row_sum = jnp.sum(exp_own, axis=0, keepdims=True) + jnp.sum(exp_other, axis=0, keepdims=True)
    own_probs, other_probs = exp_own / row_sum, exp_other / row_sum
    own_part = contract(own_values, own_probs.astype(BF16), 1, 0)
    return o_unit, o_normed, own_probs, other_probs, own_part


def finish_head(
    other_value, q_unit, k_unit, o_unit, q_normed, k_normed, o_normed,
    grad_t, own_grad_probs, own_probs, other_probs, own_part,
):
    values = dims_by_tokens(other_value).astype(BF16)
    attended = own_part + contract(values, other_probs.astype(BF16), 1, 0)
    grad_probs = contract(values, grad_t, 0, 0)
    row_dot = jnp.sum(grad_t.astype(F32) * attended, axis=0, keepdims=True)
    own_terms = (own_probs * (own_grad_probs - row_dot) * SCALE).astype(BF16)
    other_terms = (other_probs * (grad_probs - row_dot) * SCALE).astype(BF16)
    grad_query = contract(k_normed, own_terms, 1, 0) + contract(o_normed, other_terms, 1, 0)
    grad_key = contract(q_normed, own_terms, 1, 1)
    grad_other = contract(q_normed, other_terms, 1, 1)
    sums = jnp.concatenate([grad_query * q_unit, grad_key * k_unit + grad_other * o_unit], axis=0)
    return rows_of_pairs(attended).astype(BF16), jnp.sum(sums.T, axis=0, keepdims=True)


def step_offset(step):
    return ((step + 1) // 2) * (2 * (step % 2) - 1)


def relay_kernel(
    table_ref, gain_ref, qkv_rows, grad_rows, out_ref, sums_ref, qkv_ref, grad_ref,
    own_qkv, own_grad, held_keys, held_values, picked, others, notes_out, notes,
    terms_out, terms, totals_out, totals,
    own_send, own_recv, grad_send, grad_recv, held_send, held_recv,
    other_send, other_recv, note_send, note_recv,
    term_send, term_recv, total_send, total_recv,
    units, gains, normed, own_scores, own_grad_probs, probs, parts,
):
    n = held_keys.shape[0]
    replicas = totals.shape[0]
    stages = lax.axis_size("pipe")
    d, p, z = lax.axis_index("dp"), lax.axis_index("pipe"), lax.axis_index("ctx")
    ahead = lax.rem(p + 1, stages)
    behind = lax.rem(p + stages - 1, stages)

    def partner(step):
        return lax.rem(z + step_offset(step) + n, n)

    def remote(src, dst, send, recv, target):
        return pltpu.make_async_remote_copy(
            src_ref=src, dst_ref=dst, send_sem=send, recv_sem=recv,
            device_id=target, device_id_type=MESH,
        )

    barrier = pltpu.get_barrier_semaphore()

    def greet(step, carry):
        other = partner(step)
        pl.semaphore_signal(barrier, inc=1, device_id=(d, ahead, other), device_id_type=MESH)
        pl.semaphore_signal(barrier, inc=1, device_id=(d, behind, other), device_id_type=MESH)

        @pl.when(step > 0)
        def _():
            pl.semaphore_signal(barrier, inc=1, device_id=(d, p, other), device_id_type=MESH)

        return carry

    lax.fori_loop(0, n, greet, 0)
    for hop in range(1, replicas):
        pl.semaphore_signal(
            barrier, inc=1, device_id=(lax.rem(d + hop, replicas), p, z), device_id_type=MESH
        )

    width = 16 * 128

    def split_rows(index, carry):
        field, part = index // 4, lax.rem(index, 4)
        columns = pl.ds(pl.multiple_of(part * width, width), width)
        rows = pl.ds(pl.multiple_of(part * 16, 16), 16)
        qkv_ref[field, :, rows] = qkv_rows[0, 0, field, :, columns].reshape(n, 16, 128)
        return carry

    def split_grad_rows(part, carry):
        columns = pl.ds(pl.multiple_of(part * width, width), width)
        rows = pl.ds(pl.multiple_of(part * 16, 16), 16)
        grad_ref[:, rows] = grad_rows[0, 0, :, columns].reshape(n, 16, 128)
        return carry

    lax.fori_loop(0, 12, split_rows, 0)
    lax.fori_loop(0, 4, split_grad_rows, 0)
    gain_row = jnp.concatenate([gain_ref[0, 0], gain_ref[0, 1]], axis=1)

    def write_note(block, carry):
        live = jnp.where(table_ref[1, block] < n, 1.0, 0.0).astype(F32)
        notes_out[block, 0:1, :] = gain_row
        notes_out[block, 1:2, :] = jnp.full((1, 128), live, F32)
        return carry

    lax.fori_loop(0, n, write_note, 0)
    notes[z] = notes_out[z]
    pl.semaphore_wait(barrier, 3 * n - 1 + replicas - 1)

    def send_note(step, carry):
        other = partner(step)
        remote(notes_out.at[other], notes.at[z], note_send, note_recv, (d, p, other)).start()
        return carry

    held = (held_keys, held_values)

    def send_to_owner(field):
        def send(index, carry):
            other = partner(n - 1 - index)
            remote(
                qkv_ref.at[1 + field, other], held[field].at[z],
                held_send.at[field], held_recv.at[field], (d, ahead, other),
            ).start()
            return carry

        lax.fori_loop(0, n, send, 0)

    lax.fori_loop(1, n, send_note, 0)
    send_to_owner(0)
    send_to_owner(1)
    own_copy = remote(qkv_ref, own_qkv, own_send, own_recv, (d, ahead, z))
    own_copy.start()
    grad_copy = remote(grad_ref, own_grad, grad_send, grad_recv, (d, behind, z))
    grad_copy.start()
    arrivals = [
        remote(held[field], held[field], held_send.at[field], held_recv.at[field], (d, ahead, z))
        for field in range(2)
    ]

    def pick(field, block):
        listed = table_ref[1, block]
        return held[field][jnp.where(listed < n, listed, 0)]

    def send_picked(field):
        def send(index, carry):
            other = partner(lax.rem(n - index, n))
            picked[other, field] = pick(field, other)
            remote(
                picked.at[other, field], others.at[z, field],
                other_send, other_recv.at[field, z], (d, p, other),
            ).start()
            return carry

        arrivals[field].wait_recv()
        lax.fori_loop(1, n, send, 0)
        others[z, field] = pick(field, z)

    send_picked(0)
    own_copy.wait_recv()
    grad_copy.wait_recv()
    rest = pl.ds(0, n - 1)
    all_notes = remote(notes_out.at[rest], notes.at[rest], note_send, note_recv, (d, p, z))
    all_notes.wait_recv()

    def prepare(head, carry):
        (
            units[head, 0], units[head, 1], gains[head],
            normed[head, 0], normed[head, 1], normed[head, 3], normed[head, 4],
            own_scores[head], own_grad_probs[head],
        ) = prepare_head(
            own_qkv[0, head], own_qkv[1, head], own_qkv[2, head], own_grad[head],
            notes[head, 0:1, :],
        )
        return carry

    lax.fori_loop(0, n, prepare, 0)
    send_picked(1)

    def landed(field, head):
        remote(
            picked.at[head, field], others.at[head, field],
            other_send, other_recv.at[field, head], (d, p, head),
        ).wait_recv()

    def weigh(index, carry):
        head = partner(lax.rem(n - index, n))

        @pl.when(index > 0)
        def _():
            landed(0, head)

        units[head, 2], normed[head, 2], probs[head, 0], probs[head, 1], parts[head] = weigh_head(
            others[head, 0], gains[head], normed[head, 0], own_scores[head], normed[head, 3],
            notes[head, 1:2, :],
        )
        return carry

    lax.fori_loop(0, n, weigh, 0)

    def finish(index, carry):
        head = partner(lax.rem(n - index, n))

        @pl.when(index > 0)
        def _():
            landed(1, head)

        out_ref[head], terms_out[head] = finish_head(
            others[head, 1], units[head, 0], units[head, 1], units[head, 2],
            normed[head, 0], normed[head, 1], normed[head, 2], normed[head, 4],
            own_grad_probs[head], probs[head, 0], probs[head, 1], parts[head],
        )

        @pl.when(index > 0)
        def _():
            remote(terms_out.at[head], terms.at[z], term_send, term_recv, (d, p, head)).start()

        return carry

    lax.fori_loop(0, n, finish, 0)
    terms[z] = terms_out[z]
    all_terms = remote(terms_out.at[rest], terms.at[rest], term_send, term_recv, (d, p, z))
    all_terms.wait_recv()
    total = jnp.sum(terms[...], axis=0)
    totals[d] = total
    totals_out[...] = total
    for hop in range(1, replicas):
        remote(
            totals_out, totals.at[d], total_send, total_recv,
            (lax.rem(d + hop, replicas), p, z),
        ).start()
    rows = pl.ds(0, replicas - 1)
    all_totals = remote(totals.at[rows], totals.at[rows], total_send, total_recv, (d, p, z))
    all_totals.wait_recv()
    result = jnp.sum(totals[...], axis=0)
    sums_ref[0, 0] = result[:, :DIM]
    sums_ref[0, 1] = result[:, DIM:]
    own_copy.wait_send()
    grad_copy.wait_send()
    arrivals[0].wait_send()
    arrivals[1].wait_send()
    all_notes.wait_send()
    remote(picked.at[rest], picked.at[rest], other_send, other_recv.at[0, z], (d, p, z)).wait_send()
    all_terms.wait_send()
    all_totals.wait_send()


def relay(table, gains, qkv, grads):
    n = grads.shape[2]
    replicas = lax.axis_size("dp")
    dma = pltpu.SemaphoreType.DMA
    block = (ROWS, 128)
    vmem = pl.BlockSpec(memory_space=pltpu.VMEM)
    return pl.pallas_call(
        relay_kernel,
        out_shape=(
            jax.ShapeDtypeStruct((n,) + block, BF16),
            jax.ShapeDtypeStruct((1, 2, 1, DIM), F32),
        ),
        in_specs=[pl.BlockSpec(memory_space=pltpu.SMEM), vmem, vmem, vmem],
        out_specs=(vmem, vmem),
        scratch_shapes=[
            pltpu.VMEM((3, n) + block, BF16),
            pltpu.VMEM((n,) + block, BF16),
            pltpu.VMEM((3, n) + block, BF16),
            pltpu.VMEM((n,) + block, BF16),
            pltpu.VMEM((n,) + block, BF16),
            pltpu.VMEM((n,) + block, BF16),
            pltpu.VMEM((n, 2) + block, BF16),
            pltpu.VMEM((n, 2) + block, BF16),
            pltpu.VMEM((n, 2, 128), F32),
            pltpu.VMEM((n, 2, 128), F32),
            pltpu.VMEM((n, 1, 128), F32),
            pltpu.VMEM((n, 1, 128), F32),
            pltpu.VMEM((1, 128), F32),
            pltpu.VMEM((replicas, 1, 128), F32),
            dma, dma, dma, dma, dma((2,)), dma((2,)),
            dma, dma((2, n)), dma, dma,
            dma, dma, dma, dma,
            pltpu.VMEM((n, 3, DIM, 128), F32),
            pltpu.VMEM((n, DIM, 128), F32),
            pltpu.VMEM((n, 5, DIM, 128), BF16),
            pltpu.VMEM((n, 128, 128), F32),
            pltpu.VMEM((n, 128, 128), F32),
            pltpu.VMEM((n, 2, 128, 128), F32),
            pltpu.VMEM((n, DIM, 128), F32),
        ],
        compiler_params=pltpu.CompilerParams(
            collective_id=0, has_side_effects=True, vmem_limit_bytes=48 * 2**20
        ),
        cost_estimate=pl.CostEstimate(
            flops=n * 10 * 128 * 256 * DIM, bytes_accessed=n * 10 * 2**14,
            transcendentals=n * 256 * 128,
        ),
    )(table, gains, qkv, grads)


def local(activations, cotangents, norm_gains, key_blocks):
    heads = activations.shape[3]
    table = jnp.swapaxes(key_blocks[0, 0], 0, 1)
    out, sums = relay(table, norm_gains, activations, cotangents)
    return out.reshape(1, 1, heads, ROWS * 128), sums


def solution(mesh):
    return jax.shard_map(
        local,
        mesh=mesh,
        in_specs=(
            P("dp", "pipe", None, None, "ctx"),
            P("dp", "pipe", None, "ctx"),
            P("pipe", None, "ctx", None),
            P("pipe", "ctx", None, None),
        ),
        out_specs=(P("dp", "pipe", None, "ctx"), P("pipe", None, "ctx", None)),
        check_vma=False,
    )
```

```python
import jax
import jax.numpy as jnp
from jax import lax
from jax.experimental import pallas as pl
from jax.experimental.pallas import tpu as pltpu
from jax.sharding import PartitionSpec as P

DIM = 64
SCALE = DIM ** (-0.5)
ROWS = 64
EPS = 1e-06
F32 = jnp.float32
BF16 = jnp.bfloat16
MESH = pl.DeviceIdType.MESH


def dims_by_tokens(pairs):
    turned = pairs.astype(F32).T
    return jnp.concatenate([turned[:DIM], turned[DIM:]], axis=1)


def rows_of_pairs(turned):
    return jnp.concatenate([turned[:, :DIM], turned[:, DIM:]], axis=0).T


def contract(left, right, left_dim, right_dim):
    return lax.dot_general(
        left, right, (((left_dim,), (right_dim,)), ((), ())), preferred_element_type=F32
    )


def unit(vals):
    return vals * lax.rsqrt(jnp.mean(vals * vals, axis=0, keepdims=True) + EPS)


def prepare_head(query, key, value, grad, gain_row):
    gains = jnp.broadcast_to(gain_row, (2 * DIM, 2 * DIM)).T
    q_unit = unit(dims_by_tokens(query))
    k_unit = unit(dims_by_tokens(key))
    q_normed = (q_unit * gains[:DIM]).astype(BF16)
    k_normed = (k_unit * gains[DIM:]).astype(BF16)
    values = dims_by_tokens(value).astype(BF16)
    grad_t = dims_by_tokens(grad).astype(BF16)
    scores = contract(k_normed, q_normed, 0, 0) * SCALE
    grad_probs = contract(values, grad_t, 0, 0)
    return q_unit, k_unit, gains[DIM:], q_normed, k_normed, values, grad_t, scores, grad_probs


def weigh_head(other_key, key_gain, q_normed, own_scores, own_values, live_row):
    o_unit = unit(dims_by_tokens(other_key))
    o_normed = (o_unit * key_gain).astype(BF16)
    other_scores = contract(o_normed, q_normed, 0, 0) * SCALE
    other_scores = jnp.where(live_row > 0.5, other_scores, -jnp.inf)
    row_max = jnp.maximum(
        jnp.max(own_scores, axis=0, keepdims=True), jnp.max(other_scores, axis=0, keepdims=True)
    )
    exp_own = jnp.exp(own_scores - row_max)
    exp_other = jnp.exp(other_scores - row_max)
    row_sum = jnp.sum(exp_own, axis=0, keepdims=True) + jnp.sum(exp_other, axis=0, keepdims=True)
    own_probs, other_probs = exp_own / row_sum, exp_other / row_sum
    own_part = contract(own_values, own_probs.astype(BF16), 1, 0)
    return o_unit, o_normed, own_probs, other_probs, own_part


def finish_head(
    other_value, q_unit, k_unit, o_unit, q_normed, k_normed, o_normed,
    grad_t, own_grad_probs, own_probs, other_probs, own_part,
):
    values = dims_by_tokens(other_value).astype(BF16)
    attended = own_part + contract(values, other_probs.astype(BF16), 1, 0)
    grad_probs = contract(values, grad_t, 0, 0)
    row_dot = jnp.sum(grad_t.astype(F32) * attended, axis=0, keepdims=True)
    own_terms = (own_probs * (own_grad_probs - row_dot) * SCALE).astype(BF16)
    other_terms = (other_probs * (grad_probs - row_dot) * SCALE).astype(BF16)
    grad_query = contract(k_normed, own_terms, 1, 0) + contract(o_normed, other_terms, 1, 0)
    grad_key = contract(q_normed, own_terms, 1, 1)
    grad_other = contract(q_normed, other_terms, 1, 1)
    sums = jnp.concatenate([grad_query * q_unit, grad_key * k_unit + grad_other * o_unit], axis=0)
    return rows_of_pairs(attended).astype(BF16), jnp.sum(sums.T, axis=0, keepdims=True)


def step_offset(step):
    return ((step + 1) // 2) * (2 * (step % 2) - 1)


def relay_kernel(
    table_ref, gain_hbm, qkv_hbm, grad_hbm, out_ref, sums_ref,
    gain_ref, qkv_rows, grad_rows, in_sems, qkv_ref, grad_ref,
    own_qkv, own_grad, held_keys, held_values, picked, others, notes_out, notes,
    terms_out, terms, totals_out, totals,
    own_send, own_recv, grad_send, grad_recv, held_send, held_recv,
    other_send, other_recv, note_send, note_recv,
    term_send, term_recv, total_send, total_recv,
    units, gains, normed, own_scores, own_grad_probs, probs, parts,
):
    n = held_keys.shape[0]
    replicas = totals.shape[0]
    stages = lax.axis_size("pipe")
    d, p, z = lax.axis_index("dp"), lax.axis_index("pipe"), lax.axis_index("ctx")
    ahead = lax.rem(p + 1, stages)
    behind = lax.rem(p + stages - 1, stages)

    def partner(step):
        return lax.rem(z + step_offset(step) + n, n)

    def remote(src, dst, send, recv, target):
        return pltpu.make_async_remote_copy(
            src_ref=src, dst_ref=dst, send_sem=send, recv_sem=recv,
            device_id=target, device_id_type=MESH,
        )

    inputs = [
        pltpu.make_async_copy(src, dst, in_sems.at[index])
        for index, (src, dst) in enumerate(
            ((qkv_hbm, qkv_rows), (grad_hbm, grad_rows), (gain_hbm, gain_ref))
        )
    ]
    for copy in inputs:
        copy.start()
    barrier = pltpu.get_barrier_semaphore()

    def greet(index, carry):
        step = n - 1 - index
        other = partner(step)
        pl.semaphore_signal(barrier, inc=1, device_id=(d, ahead, other), device_id_type=MESH)
        pl.semaphore_signal(barrier, inc=1, device_id=(d, behind, other), device_id_type=MESH)

        @pl.when(step > 0)
        def _():
            pl.semaphore_signal(barrier, inc=1, device_id=(d, p, other), device_id_type=MESH)

        return carry

    lax.fori_loop(0, n, greet, 0)
    for hop in range(1, replicas):
        pl.semaphore_signal(
            barrier, inc=1, device_id=(lax.rem(d + hop, replicas), p, z), device_id_type=MESH
        )

    for copy in inputs:
        copy.wait()
    width = 16 * 128

    def split_rows(index, carry):
        field, part = index // 4, lax.rem(index, 4)
        columns = pl.ds(pl.multiple_of(part * width, width), width)
        rows = pl.ds(pl.multiple_of(part * 16, 16), 16)
        qkv_ref[field, :, rows] = qkv_rows[0, 0, field, :, columns].reshape(n, 16, 128)
        return carry

    def split_grad_rows(part, carry):
        columns = pl.ds(pl.multiple_of(part * width, width), width)
        rows = pl.ds(pl.multiple_of(part * 16, 16), 16)
        grad_ref[:, rows] = grad_rows[0, 0, :, columns].reshape(n, 16, 128)
        return carry

    lax.fori_loop(0, 12, split_rows, 0)
    lax.fori_loop(0, 4, split_grad_rows, 0)
    gain_row = jnp.concatenate([gain_ref[0, 0], gain_ref[0, 1]], axis=1)

    def write_note(block, carry):
        live = jnp.where(table_ref[1, block] < n, 1.0, 0.0).astype(F32)
        notes_out[block, 0:1, :] = gain_row
        notes_out[block, 1:2, :] = jnp.full((1, 128), live, F32)
        return carry

    lax.fori_loop(0, n, write_note, 0)
    notes[z] = notes_out[z]
    pl.semaphore_wait(barrier, 3 * n - 1 + replicas - 1)

    def send_note(step, carry):
        other = partner(step)
        remote(notes_out.at[other], notes.at[z], note_send, note_recv, (d, p, other)).start()
        return carry

    held = (held_keys, held_values)

    def send_to_owner(field):
        def send(index, carry):
            other = partner(n - 1 - index)
            remote(
                qkv_ref.at[1 + field, other], held[field].at[z],
                held_send.at[field], held_recv.at[field], (d, ahead, other),
            ).start()
            return carry

        lax.fori_loop(0, n, send, 0)

    lax.fori_loop(1, n, send_note, 0)
    send_to_owner(0)
    send_to_owner(1)
    own_copy = remote(qkv_ref, own_qkv, own_send, own_recv, (d, ahead, z))
    own_copy.start()
    grad_copy = remote(grad_ref, own_grad, grad_send, grad_recv, (d, behind, z))
    grad_copy.start()
    arrivals = [
        remote(held[field], held[field], held_send.at[field], held_recv.at[field], (d, ahead, z))
        for field in range(2)
    ]

    def pick(field, block):
        listed = table_ref[1, block]
        return held[field][jnp.where(listed < n, listed, 0)]

    def send_picked(field):
        def send(index, carry):
            other = partner(lax.rem(n - index, n))
            picked[other, field] = pick(field, other)
            remote(
                picked.at[other, field], others.at[z, field],
                other_send, other_recv.at[field, z], (d, p, other),
            ).start()
            return carry

        arrivals[field].wait_recv()
        lax.fori_loop(1, n, send, 0)
        others[z, field] = pick(field, z)

    send_picked(0)
    own_copy.wait_recv()
    grad_copy.wait_recv()
    rest = pl.ds(0, n - 1)
    all_notes = remote(notes_out.at[rest], notes.at[rest], note_send, note_recv, (d, p, z))
    all_notes.wait_recv()

    def prepare(head, carry):
        (
            units[head, 0], units[head, 1], gains[head],
            normed[head, 0], normed[head, 1], normed[head, 3], normed[head, 4],
            own_scores[head], own_grad_probs[head],
        ) = prepare_head(
            own_qkv[0, head], own_qkv[1, head], own_qkv[2, head], own_grad[head],
            notes[head, 0:1, :],
        )
        return carry

    lax.fori_loop(0, n, prepare, 0)
    send_picked(1)

    def landed(field, head):
        remote(
            picked.at[head, field], others.at[head, field],
            other_send, other_recv.at[field, head], (d, p, head),
        ).wait_recv()

    def weigh(index, carry):
        head = partner(lax.rem(n - index, n))

        @pl.when(index > 0)
        def _():
            landed(0, head)

        units[head, 2], normed[head, 2], probs[head, 0], probs[head, 1], parts[head] = weigh_head(
            others[head, 0], gains[head], normed[head, 0], own_scores[head], normed[head, 3],
            notes[head, 1:2, :],
        )
        return carry

    lax.fori_loop(0, n, weigh, 0)

    def finish(index, carry):
        head = partner(lax.rem(n - index, n))

        @pl.when(index > 0)
        def _():
            landed(1, head)

        out_ref[head], terms_out[head] = finish_head(
            others[head, 1], units[head, 0], units[head, 1], units[head, 2],
            normed[head, 0], normed[head, 1], normed[head, 2], normed[head, 4],
            own_grad_probs[head], probs[head, 0], probs[head, 1], parts[head],
        )

        @pl.when(index > 0)
        def _():
            remote(terms_out.at[head], terms.at[z], term_send, term_recv, (d, p, head)).start()

        return carry

    lax.fori_loop(0, n, finish, 0)
    terms[z] = terms_out[z]
    all_terms = remote(terms_out.at[rest], terms.at[rest], term_send, term_recv, (d, p, z))
    all_terms.wait_recv()
    total = jnp.sum(terms[...], axis=0)
    totals[d] = total
    totals_out[...] = total
    for hop in range(1, replicas):
        remote(
            totals_out, totals.at[d], total_send, total_recv,
            (lax.rem(d + hop, replicas), p, z),
        ).start()
    rows = pl.ds(0, replicas - 1)
    all_totals = remote(totals.at[rows], totals.at[rows], total_send, total_recv, (d, p, z))
    all_totals.wait_recv()
    result = jnp.sum(totals[...], axis=0)
    sums_ref[0, 0] = result[:, :DIM]
    sums_ref[0, 1] = result[:, DIM:]
    own_copy.wait_send()
    grad_copy.wait_send()
    arrivals[0].wait_send()
    arrivals[1].wait_send()
    all_notes.wait_send()
    remote(picked.at[rest], picked.at[rest], other_send, other_recv.at[0, z], (d, p, z)).wait_send()
    all_terms.wait_send()
    all_totals.wait_send()


def relay(table, gains, qkv, grads):
    n = grads.shape[2]
    replicas = lax.axis_size("dp")
    dma = pltpu.SemaphoreType.DMA
    block = (ROWS, 128)
    vmem = pl.BlockSpec(memory_space=pltpu.VMEM)
    hbm = pl.BlockSpec(memory_space=pl.ANY)
    return pl.pallas_call(
        relay_kernel,
        out_shape=(
            jax.ShapeDtypeStruct((n,) + block, BF16),
            jax.ShapeDtypeStruct((1, 2, 1, DIM), F32),
        ),
        in_specs=[pl.BlockSpec(memory_space=pltpu.SMEM), hbm, hbm, hbm],
        out_specs=(vmem, vmem),
        scratch_shapes=[
            pltpu.VMEM(gains.shape, F32),
            pltpu.VMEM(qkv.shape, BF16),
            pltpu.VMEM(grads.shape, BF16),
            dma((3,)),
            pltpu.VMEM((3, n) + block, BF16),
            pltpu.VMEM((n,) + block, BF16),
            pltpu.VMEM((3, n) + block, BF16),
            pltpu.VMEM((n,) + block, BF16),
            pltpu.VMEM((n,) + block, BF16),
            pltpu.VMEM((n,) + block, BF16),
            pltpu.VMEM((n, 2) + block, BF16),
            pltpu.VMEM((n, 2) + block, BF16),
            pltpu.VMEM((n, 2, 128), F32),
            pltpu.VMEM((n, 2, 128), F32),
            pltpu.VMEM((n, 1, 128), F32),
            pltpu.VMEM((n, 1, 128), F32),
            pltpu.VMEM((1, 128), F32),
            pltpu.VMEM((replicas, 1, 128), F32),
            dma, dma, dma, dma, dma((2,)), dma((2,)),
            dma, dma((2, n)), dma, dma,
            dma, dma, dma, dma,
            pltpu.VMEM((n, 3, DIM, 128), F32),
            pltpu.VMEM((n, DIM, 128), F32),
            pltpu.VMEM((n, 5, DIM, 128), BF16),
            pltpu.VMEM((n, 128, 128), F32),
            pltpu.VMEM((n, 128, 128), F32),
            pltpu.VMEM((n, 2, 128, 128), F32),
            pltpu.VMEM((n, DIM, 128), F32),
        ],
        compiler_params=pltpu.CompilerParams(
            collective_id=0, has_side_effects=True, vmem_limit_bytes=62 * 2**20
        ),
        cost_estimate=pl.CostEstimate(
            flops=n * 10 * 128 * 256 * DIM, bytes_accessed=n * 10 * 2**14,
            transcendentals=n * 256 * 128,
        ),
    )(table, gains, qkv, grads)


def local(activations, cotangents, norm_gains, key_blocks):
    heads = activations.shape[3]
    table = jnp.swapaxes(key_blocks[0, 0], 0, 1)
    out, sums = relay(table, norm_gains, activations, cotangents)
    return out.reshape(1, 1, heads, ROWS * 128), sums


def solution(mesh):
    return jax.shard_map(
        local,
        mesh=mesh,
        in_specs=(
            P("dp", "pipe", None, None, "ctx"),
            P("dp", "pipe", None, "ctx"),
            P("pipe", None, "ctx", None),
            P("pipe", "ctx", None, None),
        ),
        out_specs=(P("dp", "pipe", None, "ctx"), P("pipe", None, "ctx", None)),
        check_vma=False,
    )
```
